256 devices in a mesh: island: 4 (over z_hi, core), fsdp: 64 (over y, x, z_lo).
Axes of the slice: x: 4, y: 4, z: 8 (z_hi: 2, z_lo: 4; z = z_hi * 4 + z_lo), core: 2. Of those that a mesh axis runs over, the one named last changes fastest.
Arguments:
- activations: bfloat16 [131072, 8192], P(('island', 'fsdp')), may hold values from -6 to 6
- out_grads: bfloat16 [131072, 512], P(('island', 'fsdp')), may hold values from -0.03125 to 0.03125
- drift: float32 [4, 8192, 512], P('island', 'fsdp'), may hold values from -4 to 4
- moment_one: float32 [4, 8192, 512], P('island', 'fsdp'), may hold values from -4 to 4
- moment_two: float32 [4, 8192, 512], P('island', 'fsdp'), may hold values from 0.1 to 2
- base: float32 [8192, 512], P('fsdp'), may hold values from -6 to 6
- outer_moment: float32 [8192, 512], P('fsdp'), may hold values from -4 to 4
Outputs:
- new_base: float32 [8192, 512], P('fsdp')
- new_outer: float32 [8192, 512], P('fsdp')
- band: float32 [2048, 128], P('fsdp')
- new_one: float32 [4, 8192, 512], P('island', 'fsdp')
- new_two: float32 [4, 8192, 512], P('island', 'fsdp')
The draws below stay inside these ranges and needn't reach their ends.
All inputs are finite; a program needn't handle non-finite values.
Results may differ from the reference program's by a relative error of at most 0.0003.
Values may be sent and summed in bfloat16 or wider, within the bound.
No kernel may reach another device: no remote copies, remote signals or barrier semaphores. Data moves between devices by JAX's collectives and lax.ppermute only.
A program may use at most 128 MiB of HBM per device.

```python
import math
import jax
import jax.numpy as jnp
from jax import lax

D = 8192
KVW = 512
TOKENS = 32768
N_ISLAND = 4


def shard_levels(key, dims, shards, low, high):
    def one(axis_at, parts):
        steps = jax.random.uniform(jax.random.fold_in(jax.random.fold_in(key, 6), axis_at), (parts,), jnp.float32, low / len(shards), high / len(shards))
        return jnp.repeat(jnp.exp(steps), dims[axis_at] // parts).reshape((-1,) + (1,) * (len(dims) - axis_at - 1))

    factor_of = one(*shards[0])
    for cut in shards[1:]:
        factor_of = factor_of * one(*cut)
    return factor_of


def bell_draw(key, dims, width, most, pieces=(), kind=jnp.bfloat16):
    factor_of = shard_levels(key, dims, pieces, -0.22, 0.18) if pieces else 1.0
    values = jax.random.normal(key, dims, jnp.float32) * width * factor_of
    return jnp.minimum(jnp.maximum(values, -most), most).astype(kind)


def setup_inputs(seed: int = 0) -> dict:
    splits = jax.random.split(jax.random.key(seed), 8)
    return {
        "activations": bell_draw(splits[0], (N_ISLAND * TOKENS, D), 1.0, 6.0, ((0, 256),)),
        "out_grads": bell_draw(splits[1], (N_ISLAND * TOKENS, KVW), TOKENS ** -0.5, 0.03125, ((0, 256),)),
        "drift": bell_draw(splits[2], (N_ISLAND, D, KVW), 0.5, 4.0, ((0, 4), (1, 64)), jnp.float32),
        "moment_one": bell_draw(splits[3], (N_ISLAND, D, KVW), 0.5, 4.0, ((0, 4), (1, 64)), jnp.float32),
        "moment_two": jnp.clip(jnp.exp(math.log(2.0) - 2.9957323 * jax.random.uniform(splits[4], (N_ISLAND, D, KVW), jnp.float32) ** shard_levels(splits[4], (N_ISLAND, D, KVW), ((0, 4), (1, 64)), -0.2, 0.2)), 0.1, 2.0),
        "base": bell_draw(splits[5], (D, KVW), 1.0, 6.0, ((0, 64),), jnp.float32),
        "outer_moment": bell_draw(splits[6], (D, KVW), 0.5, 4.0, ((0, 64),), jnp.float32),
    }


def dct_band():
    freq = jnp.arange(16, dtype=jnp.float32)[:, None]
    place = jnp.arange(64, dtype=jnp.float32)[None, :]
    table = math.sqrt(2.0 / 64.0) * jnp.cos(math.pi * (2.0 * place + 1.0) * freq / 128.0)
    scale = jnp.where(jnp.arange(16)[:, None] == 0, 1.0 / math.sqrt(2.0), 1.0).astype(jnp.float32)
    return (table * scale).astype(jnp.float32)

def reference(activations, out_grads, drift, moment_one, moment_two, base, outer_moment):
    hp = lax.Precision.HIGHEST
    basis = dct_band()
    groups = drift.shape[0]
    tokens = activations.shape[0] // groups
    ones, twos, bands = ([], [], [])
    for group in range(groups):
        xs = activations[group * tokens:(group + 1) * tokens]
        gs = out_grads[group * tokens:(group + 1) * tokens]
        grad = lax.dot_general(xs, gs, (((0,), (0,)), ((), ())), preferred_element_type=jnp.float32)
        first = 0.8 * moment_one[group] + 0.2 * grad
        second = 0.95 * moment_two[group] + 0.05 * grad * grad
        step = first / (1.0 - 0.8 ** 10) / (jnp.sqrt(second / (1.0 - 0.95 ** 10)) + 1e-08)
        theta = base + drift[group]
        delta = base - (theta - 0.3 * (step + 0.1 * theta))
        tiles = delta.reshape(D // 64, 64, KVW // 64, 64)
        coeff = jnp.einsum('ka,iajb,lb->ikjl', basis, tiles, basis, precision=hp)
        bands.append(coeff.reshape(D // 4, KVW // 4))
        ones.append(first)
        twos.append(second)
    band = sum(bands) / groups
    blocks = band.reshape(D // 64, 16, KVW // 64, 16)
    smooth = jnp.einsum('ka,ikjl,lb->iajb', basis, blocks, basis, precision=hp).reshape(D, KVW)
    new_outer = 0.9 * outer_moment + smooth
    new_base = base - 0.7 * (smooth + 0.9 * new_outer)
    return (new_base, new_outer, band, jnp.stack(ones), jnp.stack(twos))
```

```python
import math

import jax
import jax.numpy as jnp
from jax import lax
from jax.sharding import PartitionSpec as P

RING = 4


def dct_band():
    freq = jnp.arange(16, dtype=jnp.float32)[:, None]
    place = jnp.arange(64, dtype=jnp.float32)[None, :]
    table = math.sqrt(2.0 / 64.0) * jnp.cos(math.pi * (2.0 * place + 1.0) * freq / 128.0)
    scale = jnp.where(jnp.arange(16)[:, None] == 0, 1.0 / math.sqrt(2.0), 1.0).astype(jnp.float32)
    return table * scale


def block_basis(width):
    return jnp.kron(jnp.eye(width // 64, dtype=jnp.float32), dct_band())


def place_index(y, x, z):
    return ((y % RING) * RING + x % RING) * RING + z % RING


def shift(value, dy=0, dx=0, dz=0):
    pairs = [
        (place_index(y, x, z), place_index(y + dy, x + dx, z + dz))
        for y in range(RING)
        for x in range(RING)
        for z in range(RING)
    ]
    return lax.ppermute(value, "fsdp", pairs)


def narrow(value):
    return value.astype(jnp.float16)


def wide(value):
    return value.astype(jnp.float32)


def pick(blocks, y, x):
    if isinstance(y, slice):
        return lax.dynamic_index_in_dim(blocks[y], x, 1, keepdims=False)
    return lax.dynamic_index_in_dim(blocks[:, x], y, 0, keepdims=False)


def first_ring(take, place, send):
    low, high = slice(0, 2), slice(2, 4)
    up = send(narrow(jnp.concatenate([take(2, low), take(1, high)])), 1)
    down = send(narrow(jnp.concatenate([take(3, low), take(2, high)])), -1)
    last_up = send(narrow(take(1, low) + wide(up[low])), 1)
    last_down = send(narrow(take(3, high) + wide(down[high])), -1)
    return jnp.concatenate(
        [
            take(0, low) + wide(down[low]) + wide(last_up),
            take(0, high) + wide(up[high]) + wide(last_down),
        ]
    )


def second_ring(total, place, send):
    out = lax.dynamic_index_in_dim(total, place, 0, keepdims=False)
    for step in (2, 1, 3):
        block = lax.dynamic_index_in_dim(total, (place + step) & 3, 0, keepdims=False)
        out = out + wide(send(narrow(block), step))
    return out


def scattered_grad(activations, out_grads):
    place = lax.axis_index("fsdp").astype(jnp.uint32)
    y, x = place >> 4, (place >> 2) & 3
    cut = out_grads.shape[1] // 2
    dims = (((0,), (0,)), ((), ()))

    def blocks(part):
        full = lax.dot_general(activations, part, dims, preferred_element_type=jnp.float32)
        return full.reshape(RING, RING, 512, cut)

    left, right = blocks(out_grads[:, :cut]), blocks(out_grads[:, cut:])
    left = first_ring(
        lambda d, half: pick(left, half, (x + d) & 3), x, lambda v, d: shift(v, dx=d)
    )
    right = first_ring(
        lambda d, half: pick(right, (y + d) & 3, half), y, lambda v, d: shift(v, dy=d)
    )
    left = second_ring(left, y, lambda v, d: shift(v, dy=d))
    right = second_ring(right, x, lambda v, d: shift(v, dx=d))
    both = narrow(jnp.concatenate([left, right], axis=1))
    groups = [[place_index(k // 4, k, z) for z in range(RING)] for k in range(16)]
    both = lax.all_to_all(both, "fsdp", 0, 0, axis_index_groups=groups, tiled=True)
    return wide(both.reshape(RING, 128, 2 * cut)).sum(0)


def island_sum(value):
    total = value
    for flip in (2, 3, 1):
        total = total + lax.ppermute(value, "island", [(k, k ^ flip) for k in range(4)])
    return total


def local(activations, out_grads, drift, moment_one, moment_two, base, outer_moment):
    hp = lax.Precision.HIGHEST
    row_count = drift.shape[1]
    col_count = drift.shape[2]
    grad = scattered_grad(activations, out_grads)
    first = 0.8 * moment_one[0] + 0.2 * grad
    second = 0.95 * moment_two[0] + 0.05 * grad * grad
    step = first / (1.0 - 0.8**10) / (jnp.sqrt(second / (1.0 - 0.95**10)) + 1e-08)
    theta = base + drift[0]
    delta = base - (theta - 0.3 * (step + 0.1 * theta))
    left_basis = block_basis(row_count)
    right_basis = block_basis(col_count)
    coeff = jnp.dot(jnp.dot(left_basis, delta, precision=hp), right_basis.T, precision=hp)
    band = island_sum(coeff) / lax.axis_size("island")
    smooth = jnp.dot(
        jnp.dot(left_basis.T, band, precision=hp), right_basis, precision=hp
    )
    new_outer = 0.9 * outer_moment + smooth
    new_base = base - 0.7 * (smooth + 0.9 * new_outer)
    return (new_base, new_outer, band, first[None], second[None])


def solution(mesh):
    in_specs = (
        P(("island", "fsdp"), None),
        P(("island", "fsdp"), None),
        P("island", "fsdp", None),
        P("island", "fsdp", None),
        P("island", "fsdp", None),
        P("fsdp", None),
        P("fsdp", None),
    )
    out_specs = (
        P("fsdp", None),
        P("fsdp", None),
        P("fsdp", None),
        P("island", "fsdp", None),
        P("island", "fsdp", None),
    )
    return jax.shard_map(local, mesh=mesh, in_specs=in_specs, out_specs=out_specs, check_vma=False)
```

```python
import functools
import math

import jax
import jax.numpy as jnp
import numpy as np
from jax import lax
from jax.experimental import pallas as pl
from jax.experimental.pallas import tpu as pltpu
from jax.sharding import PartitionSpec as P

RING = 4
HIGHEST = lax.Precision.HIGHEST


def block_basis(width):
    freq, place = np.arange(16.0)[:, None], np.arange(64.0)[None, :]
    table = math.sqrt(2.0 / 64.0) * np.cos(math.pi * (2.0 * place + 1.0) * freq / 128.0)
    table[0] /= math.sqrt(2.0)
    return np.kron(np.eye(width // 64), table).astype(np.float32)


def place_index(y, x, z):
    return ((y % RING) * RING + x % RING) * RING + z % RING


def shift(value, dy=0, dx=0, dz=0):
    pairs = [
        (place_index(y, x, z), place_index(y + dy, x + dx, z + dz))
        for y in range(RING)
        for x in range(RING)
        for z in range(RING)
    ]
    return lax.ppermute(value, "fsdp", pairs)


def narrow(value):
    return value.astype(jnp.float16)


def wide(value):
    return value.astype(jnp.float32)


def product_kernel(roles, a_ref, g_ref, *refs):
    outs, (held, flipped, raw, sems, g_sem) = refs[:4], refs[4:]
    width = held.shape[2]
    cut = flipped.shape[0] // 2
    place = lax.axis_index("fsdp")
    y, x = place >> 4, (place >> 2) & 3

    def named(half, role, j):
        low, high = roles[role]
        d = high + (low - high) * (j < 2)
        return ((y + j) & 3, (x + d) & 3) if half == 0 else ((y + d) & 3, (x + j) & 3)

    def fetch(spot):
        block = spot[0] * 4 + spot[1]
        start = pl.multiple_of(block * width, width)
        return pltpu.make_async_copy(
            a_ref.at[:, pl.ds(start, width)], held.at[block], sems.at[block]
        )

    def left(do):
        for role in range(2):
            for j in range(4):
                do(named(0, role, j))

    def rest(do):
        seen = {(j, roles[r][j // 2]) for r in range(2) for j in range(4)}
        for role in range(2):
            for j in range(4):
                if (roles[role][j // 2], j) not in seen:
                    do(named(1, role, j))

    bring = pltpu.make_async_copy(g_ref, raw, g_sem)
    bring.start()
    left(lambda spot: fetch(spot).start())
    rest(lambda spot: fetch(spot).start())
    bring.wait()
    flipped[...] = raw[...].T
    for half in range(2):
        part = flipped[:cut] if half == 0 else flipped[cut:]
        if half == 1:
            rest(lambda spot: fetch(spot).wait())

        def multiply(j, carry):
            spots = [named(half, role, j) for role in range(2)]
            if half == 0:
                for spot in spots:
                    fetch(spot).wait()
            for role, spot in enumerate(spots):
                block = held[spot[0] * 4 + spot[1]]
                product = jnp.dot(part, block, preferred_element_type=jnp.float32)
                for z in range(RING):
                    outs[2 * half + role][j, z] = product[:, z * 128 : (z + 1) * 128]
            return carry

        lax.fori_loop(0, RING, multiply, 0)


def products(activations, out_grads, roles):
    depth, rows = activations.shape
    count = RING * RING
    cut = out_grads.shape[1] // 2
    part = jax.ShapeDtypeStruct((RING, RING, cut, rows // count // RING), jnp.float32)
    return pl.pallas_call(
        functools.partial(product_kernel, roles),
        in_specs=[pl.BlockSpec(memory_space=pl.ANY)] * 2,
        out_specs=[pl.BlockSpec(memory_space=pltpu.VMEM)] * 4,
        out_shape=[part] * 4,
        scratch_shapes=[
            pltpu.VMEM((count, depth, rows // count), activations.dtype),
            pltpu.VMEM(out_grads.shape[::-1], out_grads.dtype),
            pltpu.VMEM(out_grads.shape, out_grads.dtype),
            pltpu.SemaphoreType.DMA((count,)),
            pltpu.SemaphoreType.DMA,
        ],
        compiler_params=pltpu.CompilerParams(vmem_limit_bytes=50 << 20),
        cost_estimate=pl.CostEstimate(
            flops=2 * rows * cut * depth, bytes_accessed=depth * rows * 2, transcendentals=0
        ),
    )(activations, out_grads)


def scattered_grad(activations, out_grads):
    sends = products(activations, out_grads, ((2, 1), (3, 2)))
    keeps = products(activations, out_grads, ((1, 3), (0, 0)))

    def along(path, value, d):
        return shift(value, dx=d) if path == 0 else shift(value, dy=d)

    def across(path, value, d):
        return shift(value, dy=d) if path == 0 else shift(value, dx=d)

    up = [along(p, narrow(sends[2 * p]), 1) for p in (0, 1)]
    down = [along(p, narrow(sends[2 * p + 1]), -1) for p in (0, 1)]
    sums = []
    for p in (0, 1):
        near, own = keeps[2 * p], keeps[2 * p + 1]
        low = along(p, narrow(near[:2] + wide(up[p][:2])), 1)
        high = along(p, narrow(near[2:] + wide(down[p][2:])), -1)
        low = own[:2] + wide(down[p][:2]) + wide(low)
        high = own[2:] + wide(up[p][2:]) + wide(high)
        total = low[0]
        for value, d in ((high[0], 2), (low[1], 1), (high[1], 3)):
            total = total + wide(across(p, narrow(value), d))
        sums.append(total)
    both = narrow(jnp.concatenate(sums, axis=1))
    groups = [[place_index(k // 4, k, z) for z in range(RING)] for k in range(16)]
    both = lax.all_to_all(both, "fsdp", 0, 0, axis_index_groups=groups, tiled=True)
    return wide(both).sum(0)


def step_kernel(grad_ref, drift, one, two, base, rows, cols, new_one, new_two, coeff):
    grad = grad_ref[...].T
    first = 0.8 * one[...] + 0.2 * grad
    second = 0.95 * two[...] + 0.05 * grad * grad
    new_one[...] = first
    new_two[...] = second
    step = first / (1.0 - 0.8**10) / (jnp.sqrt(second / (1.0 - 0.95**10)) + 1e-08)
    theta = base[...] + drift[...]
    delta = base[...] - (theta - 0.3 * (step + 0.1 * theta))
    inner = jnp.dot(rows[...], delta, precision=HIGHEST, preferred_element_type=jnp.float32)
    coeff[...] = lax.dot_general(
        inner, cols[...], (((1,), (1,)), ((), ())), precision=HIGHEST,
        preferred_element_type=jnp.float32,
    )


def outer_kernel(coeffs, base, moment, rows, cols, new_base, new_outer, band_ref):
    band = jnp.sum(coeffs[...], axis=0) / coeffs.shape[0]
    band_ref[...] = band
    inner = lax.dot_general(
        rows[...], band, (((0,), (0,)), ((), ())), precision=HIGHEST,
        preferred_element_type=jnp.float32,
    )
    smooth = jnp.dot(inner, cols[...], precision=HIGHEST, preferred_element_type=jnp.float32)
    outer = 0.9 * moment[...] + smooth
    new_outer[...] = outer
    new_base[...] = base[...] - 0.7 * (smooth + 0.9 * outer)


def on_chip(kernel, shapes, *args):
    return pl.pallas_call(
        kernel,
        in_specs=[pl.BlockSpec(memory_space=pltpu.VMEM)] * len(args),
        out_specs=[pl.BlockSpec(memory_space=pltpu.VMEM)] * len(shapes),
        out_shape=[jax.ShapeDtypeStruct(shape, jnp.float32) for shape in shapes],
    )(*args)


def every_island(value):
    return lax.all_gather(value, "island")


def local(activations, out_grads, drift, moment_one, moment_two, base, outer_moment):
    rows, cols = block_basis(drift.shape[1]), block_basis(drift.shape[2])
    grad = scattered_grad(activations, out_grads)
    full, small = drift.shape[1:], (rows.shape[0], cols.shape[0])
    first, second, coeff = on_chip(
        step_kernel, [full, full, small],
        grad, drift[0], moment_one[0], moment_two[0], base, rows, cols,
    )
    new_base, new_outer, band = on_chip(
        outer_kernel, [full, full, small], every_island(coeff), base, outer_moment, rows, cols
    )
    return (new_base, new_outer, band, first[None], second[None])


def solution(mesh):
    in_specs = (
        P(("island", "fsdp"), None),
        P(("island", "fsdp"), None),
        P("island", "fsdp", None),
        P("island", "fsdp", None),
        P("island", "fsdp", None),
        P("fsdp", None),
        P("fsdp", None),
    )
    out_specs = (
        P("fsdp", None),
        P("fsdp", None),
        P("fsdp", None),
        P("island", "fsdp", None),
        P("island", "fsdp", None),
    )
    return jax.shard_map(local, mesh=mesh, in_specs=in_specs, out_specs=out_specs, check_vma=False)
```

```python
import functools
import math

import jax
import jax.numpy as jnp
import numpy as np
from jax import lax
from jax.experimental import pallas as pl
from jax.experimental.pallas import tpu as pltpu
from jax.sharding import PartitionSpec as P

RING = 4
SCALE = 8.0
HIGHEST = lax.Precision.HIGHEST


def block_basis(width):
    freq, place = np.arange(16.0)[:, None], np.arange(64.0)[None, :]
    table = math.sqrt(2.0 / 64.0) * np.cos(math.pi * (2.0 * place + 1.0) * freq / 128.0)
    table[0] /= math.sqrt(2.0)
    return np.kron(np.eye(width // 64), table).astype(np.float32)


def place_index(y, x, z):
    return ((y % RING) * RING + x % RING) * RING + z % RING


def shift(value, dy=0, dx=0, dz=0):
    pairs = [
        (place_index(y, x, z), place_index(y + dy, x + dx, z + dz))
        for y in range(RING)
        for x in range(RING)
        for z in range(RING)
    ]
    return lax.ppermute(value, "fsdp", pairs)


def narrow(value):
    return value.astype(jnp.float16)


def wide(value):
    return value.astype(jnp.float32)


def product_kernel(roles, unroll, a_ref, g_ref, *refs):
    outs, (held, flipped, raw, sems, g_sem) = refs[:4], refs[4:]
    width = held.shape[2]
    cut = flipped.shape[0] // 2
    place = lax.axis_index("fsdp")
    y, x, z = place >> 4, (place >> 2) & 3, place & 3

    def named(half, role, j):
        low, high = roles[role]
        d = high + (low - high) * (j < 2)
        return ((y + j) & 3, (x + d) & 3) if half == 0 else ((y + d) & 3, (x + j) & 3)

    def fetch(spot):
        block = spot[0] * 4 + spot[1]
        start = pl.multiple_of(block * width, width)
        return pltpu.make_async_copy(
            a_ref.at[:, pl.ds(start, width)], held.at[block], sems.at[block]
        )

    def left(do):
        for role in range(2):
            for j in range(4):
                do(named(0, role, j))

    def rest(do):
        seen = {(j, roles[r][j // 2]) for r in range(2) for j in range(4)}
        for role in range(2):
            for j in range(4):
                if (roles[role][j // 2], j) not in seen:
                    do(named(1, role, j))

    bring = pltpu.make_async_copy(g_ref, raw, g_sem)
    bring.start()
    left(lambda spot: fetch(spot).start())
    rest(lambda spot: fetch(spot).start())
    bring.wait()
    flipped[...] = raw[...].T * SCALE
    for half in range(2):
        part = flipped[:cut] if half == 0 else flipped[cut:]
        if half == 1:
            rest(lambda spot: fetch(spot).wait())

        def multiply(j, carry):
            spots = [named(half, role, j) for role in range(2)]
            if half == 0:
                for spot in spots:
                    fetch(spot).wait()
            for role, spot in enumerate(spots):
                block = held[spot[0] * 4 + spot[1]]
                product = jnp.dot(part, block, preferred_element_type=jnp.float32)
                for k in range(RING):
                    outs[2 * half + role][j, k ^ z] = product[:, k * 128 : (k + 1) * 128]
            return carry

        lax.fori_loop(0, RING, multiply, 0, unroll=unroll)


def products(activations, out_grads, roles, unroll):
    depth, rows = activations.shape
    count = RING * RING
    cut = out_grads.shape[1] // 2
    part = jax.ShapeDtypeStruct((RING, RING, cut, rows // count // RING), jnp.float32)
    return pl.pallas_call(
        functools.partial(product_kernel, roles, unroll),
        in_specs=[pl.BlockSpec(memory_space=pl.ANY)] * 2,
        out_specs=[pl.BlockSpec(memory_space=pltpu.VMEM)] * 4,
        out_shape=[part] * 4,
        scratch_shapes=[
            pltpu.VMEM((count, depth, rows // count), activations.dtype),
            pltpu.VMEM(out_grads.shape[::-1], out_grads.dtype),
            pltpu.VMEM(out_grads.shape, out_grads.dtype),
            pltpu.SemaphoreType.DMA((count,)),
            pltpu.SemaphoreType.DMA,
        ],
        compiler_params=pltpu.CompilerParams(vmem_limit_bytes=44 << 20),
        cost_estimate=pl.CostEstimate(
            flops=2 * rows * cut * depth, bytes_accessed=depth * rows * 2, transcendentals=0
        ),
    )(activations, out_grads)


def scattered_grad(activations, out_grads):
    sends = products(activations, out_grads, ((2, 1), (3, 2)), RING)
    keeps = products(activations, out_grads, ((1, 3), (0, 0)), 1)

    def along(path, value, d):
        return shift(value, dx=d) if path == 0 else shift(value, dy=d)

    def across(path, value, d):
        return shift(value, dy=d) if path == 0 else shift(value, dx=d)

    up = [along(p, narrow(sends[2 * p]), 1) for p in (0, 1)]
    down = [along(p, narrow(sends[2 * p + 1]), -1) for p in (0, 1)]
    sums = []
    for p in (0, 1):
        near, own = keeps[2 * p], keeps[2 * p + 1]
        low = along(p, narrow(near[:2] + wide(up[p][:2])), 1)
        high = along(p, narrow(near[2:] + wide(down[p][2:])), -1)
        low = own[:2] + wide(down[p][:2]) + wide(low)
        high = own[2:] + wide(up[p][2:]) + wide(high)
        total = low[0]
        for value, d in ((high[0], 2), (low[1], 1), (high[1], 3)):
            total = total + wide(across(p, narrow(value), d))
        part = total[0]
        for flip in (2, 3, 1):
            pairs = [(k, k ^ flip) for k in range(RING**3)]
            part = part + wide(lax.ppermute(narrow(total[flip]), "fsdp", pairs))
        sums.append(part)
    return sums


def moments(left, right, one, two):
    grad = jnp.concatenate([left[...], right[...]]).T * (1.0 / SCALE)
    return 0.8 * one[...] + 0.2 * grad, 0.95 * two[...] + 0.05 * grad * grad


def moment_kernel(left, right, one, two, new_one, new_two):
    new_one[...], new_two[...] = moments(left, right, one, two)


def band_kernel(left, right, one, two, drift, base, rows, cols, coeff):
    first, second = moments(left, right, one, two)
    step = first / (1.0 - 0.8**10) / (jnp.sqrt(second / (1.0 - 0.95**10)) + 1e-08)
    theta = base[...] + drift[...]
    delta = base[...] - (theta - 0.3 * (step + 0.1 * theta))
    inner = jnp.dot(rows[...], delta, precision=HIGHEST, preferred_element_type=jnp.float32)
    coeff[...] = lax.dot_general(
        inner, cols[...], (((1,), (1,)), ((), ())), precision=HIGHEST,
        preferred_element_type=jnp.float32,
    )


def outer_kernel(here, there, base, moment, rows, cols, new_base, new_outer, band_ref):
    band = (here[...] + there[...]) / 4.0
    band_ref[...] = band
    inner = lax.dot_general(
        rows[...], band, (((0,), (0,)), ((), ())), precision=HIGHEST,
        preferred_element_type=jnp.float32,
    )
    smooth = jnp.dot(inner, cols[...], precision=HIGHEST, preferred_element_type=jnp.float32)
    outer = 0.9 * moment[...] + smooth
    new_outer[...] = outer
    new_base[...] = base[...] - 0.7 * (smooth + 0.9 * outer)


def on_chip(kernel, shapes, *args):
    return pl.pallas_call(
        kernel,
        in_specs=[pl.BlockSpec(memory_space=pltpu.VMEM)] * len(args),
        out_specs=[pl.BlockSpec(memory_space=pltpu.VMEM)] * len(shapes),
        out_shape=[jax.ShapeDtypeStruct(shape, jnp.float32) for shape in shapes],
    )(*args)


def flipped_island(value, flip):
    return lax.ppermute(value, "island", [(k, k ^ flip) for k in range(4)])


def local(activations, out_grads, drift, moment_one, moment_two, base, outer_moment):
    rows, cols = block_basis(drift.shape[1]), block_basis(drift.shape[2])
    left, right = scattered_grad(activations, out_grads)
    full, small = drift.shape[1:], (rows.shape[0], cols.shape[0])
    state = left, right, moment_one[0], moment_two[0]
    (coeff,) = on_chip(band_kernel, [small], *state, drift[0], base, rows, cols)
    chip = coeff + flipped_island(coeff, 1)
    there = flipped_island(chip, 2)
    first, second = on_chip(moment_kernel, [full, full], *state)
    new_base, new_outer, band = on_chip(
        outer_kernel, [full, full, small], chip, there, base, outer_moment, rows, cols
    )
    return (new_base, new_outer, band, first[None], second[None])


def solution(mesh):
    in_specs = (
        P(("island", "fsdp"), None),
        P(("island", "fsdp"), None),
        P("island", "fsdp", None),
        P("island", "fsdp", None),
        P("island", "fsdp", None),
        P("fsdp", None),
        P("fsdp", None),
    )
    out_specs = (
        P("fsdp", None),
        P("fsdp", None),
        P("fsdp", None),
        P("island", "fsdp", None),
        P("island", "fsdp", None),
    )
    return jax.shard_map(local, mesh=mesh, in_specs=in_specs, out_specs=out_specs, check_vma=False)
```

```python
import functools
import math

import jax
import jax.numpy as jnp
import numpy as np
from jax import lax
from jax.experimental import pallas as pl
from jax.experimental.pallas import tpu as pltpu
from jax.sharding import PartitionSpec as P

RING = 4
SCALE = 8.0
HIGHEST = lax.Precision.HIGHEST


def block_basis(width):
    freq, place = np.arange(16.0)[:, None], np.arange(64.0)[None, :]
    table = math.sqrt(2.0 / 64.0) * np.cos(math.pi * (2.0 * place + 1.0) * freq / 128.0)
    table[0] /= math.sqrt(2.0)
    return np.kron(np.eye(width // 64), table).astype(np.float32)


def place_index(y, x, z):
    return ((y % RING) * RING + x % RING) * RING + z % RING


def shift(value, dy=0, dx=0, dz=0):
    pairs = [
        (place_index(y, x, z), place_index(y + dy, x + dx, z + dz))
        for y in range(RING)
        for x in range(RING)
        for z in range(RING)
    ]
    return lax.ppermute(value, "fsdp", pairs)


def narrow(value):
    return value.astype(jnp.float16)


def wide(value):
    return value.astype(jnp.float32)


def product_kernel(roles, unroll, a_ref, g_ref, *refs):
    outs, (held, flipped, raw, sems, g_sem) = refs[:4], refs[4:]
    width = held.shape[2]
    cut = flipped.shape[0] // 2
    place = lax.axis_index("fsdp")
    y, x, z = place >> 4, (place >> 2) & 3, place & 3

    def named(half, role, j):
        low, high = roles[role]
        d = high + (low - high) * (j < 2)
        return ((y + j) & 3, (x + d) & 3) if half == 0 else ((y + d) & 3, (x + j) & 3)

    def fetch(spot):
        block = spot[0] * 4 + spot[1]
        start = pl.multiple_of(block * width, width)
        return pltpu.make_async_copy(
            a_ref.at[:, pl.ds(start, width)], held.at[block], sems.at[block]
        )

    def left(do):
        for role in range(2):
            for j in range(4):
                do(named(0, role, j))

    def rest(do):
        seen = {(j, roles[r][j // 2]) for r in range(2) for j in range(4)}
        for role in range(2):
            for j in range(4):
                if (roles[role][j // 2], j) not in seen:
                    do(named(1, role, j))

    bring = pltpu.make_async_copy(g_ref, raw, g_sem)
    bring.start()
    left(lambda spot: fetch(spot).start())
    rest(lambda spot: fetch(spot).start())
    bring.wait()
    flipped[...] = raw[...].T * SCALE
    for half in range(2):
        part = flipped[:cut] if half == 0 else flipped[cut:]
        if half == 1:
            rest(lambda spot: fetch(spot).wait())

        def multiply(j, carry):
            spots = [named(half, role, j) for role in range(2)]
            if half == 0:
                for spot in spots:
                    fetch(spot).wait()
            for role, spot in enumerate(spots):
                block = held[spot[0] * 4 + spot[1]]
                product = jnp.dot(part, block, preferred_element_type=jnp.float32)
                for k in range(RING):
                    outs[2 * half + role][j, k ^ z] = product[:, k * 128 : (k + 1) * 128]
            return carry

        lax.fori_loop(0, RING, multiply, 0, unroll=unroll)


def products(activations, out_grads, roles, unroll):
    depth, rows = activations.shape
    count = RING * RING
    cut = out_grads.shape[1] // 2
    part = jax.ShapeDtypeStruct((RING, RING, cut, rows // count // RING), jnp.float32)
    return pl.pallas_call(
        functools.partial(product_kernel, roles, unroll),
        in_specs=[pl.BlockSpec(memory_space=pl.ANY)] * 2,
        out_specs=[pl.BlockSpec(memory_space=pltpu.VMEM)] * 4,
        out_shape=[part] * 4,
        scratch_shapes=[
            pltpu.VMEM((count, depth, rows // count), activations.dtype),
            pltpu.VMEM(out_grads.shape[::-1], out_grads.dtype),
            pltpu.VMEM(out_grads.shape, out_grads.dtype),
            pltpu.SemaphoreType.DMA((count,)),
            pltpu.SemaphoreType.DMA,
        ],
        compiler_params=pltpu.CompilerParams(vmem_limit_bytes=44 << 20),
        cost_estimate=pl.CostEstimate(
            flops=2 * rows * cut * depth, bytes_accessed=depth * rows * 2, transcendentals=0
        ),
    )(activations, out_grads)


def scattered_grad(activations, out_grads):
    sends = products(activations, out_grads, ((2, 1), (3, 2)), RING)
    keeps = products(activations, out_grads, ((1, 3), (0, 0)), 1)

    def along(path, value, d):
        return shift(value, dx=d) if path == 0 else shift(value, dy=d)

    def across(path, value, d):
        return shift(value, dy=d) if path == 0 else shift(value, dx=d)

    up = [along(p, narrow(sends[2 * p]), 1) for p in (0, 1)]
    down = [along(p, narrow(sends[2 * p + 1]), -1) for p in (0, 1)]
    sums = []
    for p in (0, 1):
        near, own = keeps[2 * p], keeps[2 * p + 1]
        low = along(p, narrow(near[:2] + wide(up[p][:2])), 1)
        high = along(p, narrow(near[2:] + wide(down[p][2:])), -1)
        low = own[:2] + wide(down[p][:2]) + wide(low)
        high = own[2:] + wide(up[p][2:]) + wide(high)
        total = low[0]
        for value, d in ((high[0], 2), (low[1], 1), (high[1], 3)):
            total = total + wide(across(p, narrow(value), d))
        part = total[0]
        for flip in (2, 3, 1):
            pairs = [(k, k ^ flip) for k in range(RING**3)]
            part = part + wide(lax.ppermute(narrow(total[flip]), "fsdp", pairs))
        sums.append(part)
    return sums


def moments(left, right, one, two):
    grad = jnp.concatenate([left[...], right[...]]).T * (1.0 / SCALE)
    return 0.8 * one[...] + 0.2 * grad, 0.95 * two[...] + 0.05 * grad * grad


def moment_kernel(left, right, one, two, new_one, new_two):
    new_one[...], new_two[...] = moments(left, right, one, two)


def band_kernel(left, right, one, two, drift, base, rows, cols, coeff):
    first, second = moments(left, right, one, two)
    step = first / (1.0 - 0.8**10) / (jnp.sqrt(second / (1.0 - 0.95**10)) + 1e-08)
    theta = base[...] + drift[...]
    delta = base[...] - (theta - 0.3 * (step + 0.1 * theta))
    inner = jnp.dot(rows[...], delta, precision=HIGHEST, preferred_element_type=jnp.float32)
    coeff[...] = lax.dot_general(
        inner, cols[...], (((1,), (1,)), ((), ())), precision=HIGHEST,
        preferred_element_type=jnp.float32,
    )


def outer_kernel(here, there, base, moment, rows, cols, new_base, new_outer, band_ref):
    band = (here[...] + there[...]) / 4.0
    band_ref[...] = band
    inner = lax.dot_general(
        rows[...], band, (((0,), (0,)), ((), ())), precision=HIGHEST,
        preferred_element_type=jnp.float32,
    )
    smooth = jnp.dot(inner, cols[...], precision=HIGHEST, preferred_element_type=jnp.float32)
    outer = 0.9 * moment[...] + smooth
    new_outer[...] = outer
    new_base[...] = base[...] - 0.7 * (smooth + 0.9 * outer)


def on_chip(kernel, shapes, *args):
    return pl.pallas_call(
        kernel,
        in_specs=[pl.BlockSpec(memory_space=pltpu.VMEM)] * len(args),
        out_specs=[pl.BlockSpec(memory_space=pltpu.VMEM)] * len(shapes),
        out_shape=[jax.ShapeDtypeStruct(shape, jnp.float32) for shape in shapes],
        compiler_params=pltpu.CompilerParams(vmem_limit_bytes=8 << 20),
    )(*args)


def flipped_island(value, flip):
    return lax.ppermute(value, "island", [(k, k ^ flip) for k in range(4)])


def local(activations, out_grads, drift, moment_one, moment_two, base, outer_moment):
    rows, cols = block_basis(drift.shape[1]), block_basis(drift.shape[2])
    left, right = scattered_grad(activations, out_grads)
    full, small = drift.shape[1:], (rows.shape[0], cols.shape[0])
    state = left, right, moment_one[0], moment_two[0]
    (coeff,) = on_chip(band_kernel, [small], *state, drift[0], base, rows, cols)
    chip = coeff + flipped_island(coeff, 1)
    there = flipped_island(chip, 2)
    first, second = on_chip(moment_kernel, [full, full], *state)
    new_base, new_outer, band = on_chip(
        outer_kernel, [full, full, small], chip, there, base, outer_moment, rows, cols
    )
    return (new_base, new_outer, band, first[None], second[None])


def solution(mesh):
    in_specs = (
        P(("island", "fsdp"), None),
        P(("island", "fsdp"), None),
        P("island", "fsdp", None),
        P("island", "fsdp", None),
        P("island", "fsdp", None),
        P("fsdp", None),
        P("fsdp", None),
    )
    out_specs = (
        P("fsdp", None),
        P("fsdp", None),
        P("fsdp", None),
        P("island", "fsdp", None),
        P("island", "fsdp", None),
    )
    return jax.shard_map(local, mesh=mesh, in_specs=in_specs, out_specs=out_specs, check_vma=False)
```

```python
import functools
import math

import jax
import jax.numpy as jnp
import numpy as np
from jax import lax
from jax.experimental import pallas as pl
from jax.experimental.pallas import tpu as pltpu
from jax.sharding import PartitionSpec as P

RING = 4
SCALE = 8.0
HIGHEST = lax.Precision.HIGHEST


def block_basis(width):
    freq, place = np.arange(16.0)[:, None], np.arange(64.0)[None, :]
    table = math.sqrt(2.0 / 64.0) * np.cos(math.pi * (2.0 * place + 1.0) * freq / 128.0)
    table[0] /= math.sqrt(2.0)
    return np.kron(np.eye(width // 64), table).astype(np.float32)


def place_index(y, x, z):
    return ((y % RING) * RING + x % RING) * RING + z % RING


def shift(value, dy=0, dx=0, dz=0):
    pairs = [
        (place_index(y, x, z), place_index(y + dy, x + dx, z + dz))
        for y in range(RING)
        for x in range(RING)
        for z in range(RING)
    ]
    return lax.ppermute(value, "fsdp", pairs)


def narrow(value):
    return value.astype(jnp.float16)


def wide(value):
    return value.astype(jnp.float32)


FAR_UP, FAR_DOWN = ((2, 0), (2, 1)), ((2, 2), (2, 3))
UP, DOWN, OWN = (tuple((d, j) for j in range(RING)) for d in (1, 3, 0))


def places(half, block):
    return block[::-1] if half == 0 else block


def product_kernel(plan, a_ref, g_ref, *refs):
    outs, (held, turned, raw, sems, g_sem) = refs[: len(plan)], refs[len(plan) :]
    width = held.shape[2]
    cut = turned.shape[0] // 2
    place = lax.axis_index("fsdp")
    y, x, z = place >> 4, (place >> 2) & 3, place & 3
    order = list(dict.fromkeys(places(half, block) for half, blocks in plan for block in blocks))

    def fetch(slot):
        up_y, up_x = order[slot]
        start = pl.multiple_of((((y + up_y) & 3) * RING + ((x + up_x) & 3)) * width, width)
        return pltpu.make_async_copy(
            a_ref.at[:, pl.ds(start, width)], held.at[slot], sems.at[slot]
        )

    bring = pltpu.make_async_copy(g_ref, raw, g_sem)
    bring.start()
    for slot in range(len(order)):
        fetch(slot).start()
    bring.wait()
    turned[...] = raw[...].T * SCALE
    ready = 0
    for out, (half, blocks) in zip(outs, plan):
        part = turned[half * cut : (half + 1) * cut]
        for k, block in enumerate(blocks):
            slot = order.index(places(half, block))
            while ready <= slot:
                fetch(ready).wait()
                ready += 1
            product = jnp.dot(part, held[slot], preferred_element_type=jnp.float32)
            for to in range(RING):
                out[k, to ^ z] = product[:, to * 128 : (to + 1) * 128]


def products(activations, out_grads, *kinds, vmem):
    plan = [(half, blocks) for half in (0, 1) for blocks in kinds]
    depth, rows = activations.shape
    width, cut = rows // RING**2, out_grads.shape[1] // 2
    count = len({places(half, block) for half, blocks in plan for block in blocks})
    total = sum(len(blocks) for _, blocks in plan)
    outs = pl.pallas_call(
        functools.partial(product_kernel, plan),
        in_specs=[pl.BlockSpec(memory_space=pl.ANY)] * 2,
        out_specs=[pl.BlockSpec(memory_space=pltpu.VMEM)] * len(plan),
        out_shape=[
            jax.ShapeDtypeStruct((len(blocks), RING, cut, width // RING), jnp.float32)
            for _, blocks in plan
        ],
        scratch_shapes=[
            pltpu.VMEM((count, depth, width), activations.dtype),
            pltpu.VMEM(out_grads.shape[::-1], out_grads.dtype),
            pltpu.VMEM(out_grads.shape, out_grads.dtype),
            pltpu.SemaphoreType.DMA((count,)),
            pltpu.SemaphoreType.DMA,
        ],
        compiler_params=pltpu.CompilerParams(vmem_limit_bytes=vmem << 20),
        cost_estimate=pl.CostEstimate(
            flops=2 * total * width * cut * depth,
            bytes_accessed=count * depth * width * 2,
            transcendentals=0,
        ),
    )(activations, out_grads)
    return outs[: len(kinds)], outs[len(kinds) :]


def block_sum(terms, k):
    out = wide(terms[0][k])
    for value in terms[1:]:
        out = out + wide(value[k])
    return out


def scattered_grad(activations, out_grads):
    halves = (0, 1)
    far = products(activations, out_grads, FAR_UP, FAR_DOWN, vmem=49)
    near = products(activations, out_grads, UP, DOWN, vmem=44)
    own = products(activations, out_grads, OWN, vmem=44)

    def along(half, value, d):
        return shift(value, dx=d) if half == 0 else shift(value, dy=d)

    def across(half, value, d):
        return shift(value, dy=d) if half == 0 else shift(value, dx=d)

    first = [(along(h, narrow(far[h][0]), 1), along(h, narrow(far[h][1]), -1)) for h in halves]
    sums = []
    for h in halves:
        up, down = near[h]
        below, above = first[h]
        pads = ((0, 0, 0),) * 3
        zero = jnp.zeros((), jnp.float16)
        up = narrow(up + wide(lax.pad(below, zero, ((0, 2, 0),) + pads)))
        down = narrow(down + wide(lax.pad(above, zero, ((2, 0, 0),) + pads)))
        terms = own[h][0], along(h, up, 1), along(h, down, -1)
        sent = [across(h, narrow(block_sum(terms, d)), d) for d in (1, 3, 2)]
        terms = [block_sum(terms, 0)] + sent
        sent = []
        for flip in (2, 3, 1):
            pairs = [(k, k ^ flip) for k in range(RING**3)]
            sent.append(lax.ppermute(narrow(block_sum(terms, flip)), "fsdp", pairs))
        out = block_sum(terms, 0)
        for value in sent:
            out = out + wide(value)
        sums.append(out)
    return sums


def moments(left, right, one, two):
    grad = jnp.concatenate([left[...], right[...]]).T * (1.0 / SCALE)
    return 0.8 * one[...] + 0.2 * grad, 0.95 * two[...] + 0.05 * grad * grad


def moment_kernel(left, right, one, two, new_one, new_two):
    new_one[...], new_two[...] = moments(left, right, one, two)


def band_kernel(left, right, one, two, drift, base, rows, cols, coeff):
    first, second = moments(left, right, one, two)
    step = first / (1.0 - 0.8**10) / (jnp.sqrt(second / (1.0 - 0.95**10)) + 1e-08)
    theta = base[...] + drift[...]
    delta = base[...] - (theta - 0.3 * (step + 0.1 * theta))
    inner = jnp.dot(rows[...], delta, precision=HIGHEST, preferred_element_type=jnp.float32)
    coeff[...] = lax.dot_general(
        inner, cols[...], (((1,), (1,)), ((), ())), precision=HIGHEST,
        preferred_element_type=jnp.float32,
    )


def outer_kernel(here, there, base, moment, rows, cols, new_base, new_outer, band_ref):
    band = (here[...] + there[...]) / 4.0
    band_ref[...] = band
    inner = lax.dot_general(
        rows[...], band, (((0,), (0,)), ((), ())), precision=HIGHEST,
        preferred_element_type=jnp.float32,
    )
    smooth = jnp.dot(inner, cols[...], precision=HIGHEST, preferred_element_type=jnp.float32)
    outer = 0.9 * moment[...] + smooth
    new_outer[...] = outer
    new_base[...] = base[...] - 0.7 * (smooth + 0.9 * outer)


def on_chip(kernel, shapes, *args):
    return pl.pallas_call(
        kernel,
        in_specs=[pl.BlockSpec(memory_space=pltpu.VMEM)] * len(args),
        out_specs=[pl.BlockSpec(memory_space=pltpu.VMEM)] * len(shapes),
        out_shape=[jax.ShapeDtypeStruct(shape, jnp.float32) for shape in shapes],
        compiler_params=pltpu.CompilerParams(vmem_limit_bytes=8 << 20),
    )(*args)


def flipped_island(value, flip):
    return lax.ppermute(value, "island", [(k, k ^ flip) for k in range(4)])


def local(activations, out_grads, drift, moment_one, moment_two, base, outer_moment):
    rows, cols = block_basis(drift.shape[1]), block_basis(drift.shape[2])
    left, right = scattered_grad(activations, out_grads)
    full, small = drift.shape[1:], (rows.shape[0], cols.shape[0])
    state = left, right, moment_one[0], moment_two[0]
    (coeff,) = on_chip(band_kernel, [small], *state, drift[0], base, rows, cols)
    chip = coeff + flipped_island(coeff, 1)
    there = flipped_island(chip, 2)
    first, second = on_chip(moment_kernel, [full, full], *state)
    new_base, new_outer, band = on_chip(
        outer_kernel, [full, full, small], chip, there, base, outer_moment, rows, cols
    )
    return (new_base, new_outer, band, first[None], second[None])


def solution(mesh):
    in_specs = (
        P(("island", "fsdp"), None),
        P(("island", "fsdp"), None),
        P("island", "fsdp", None),
        P("island", "fsdp", None),
        P("island", "fsdp", None),
        P("fsdp", None),
        P("fsdp", None),
    )
    out_specs = (
        P("fsdp", None),
        P("fsdp", None),
        P("fsdp", None),
        P("island", "fsdp", None),
        P("island", "fsdp", None),
    )
    return jax.shard_map(local, mesh=mesh, in_specs=in_specs, out_specs=out_specs, check_vma=False)
```

```python
import functools
import math

import jax
import jax.numpy as jnp
import numpy as np
from jax import lax
from jax.experimental import pallas as pl
from jax.experimental.pallas import tpu as pltpu
from jax.sharding import PartitionSpec as P

RING = 4
SCALE = 8.0
HIGHEST = lax.Precision.HIGHEST


def block_basis(width):
    freq, place = np.arange(16.0)[:, None], np.arange(64.0)[None, :]
    table = math.sqrt(2.0 / 64.0) * np.cos(math.pi * (2.0 * place + 1.0) * freq / 128.0)
    table[0] /= math.sqrt(2.0)
    return np.kron(np.eye(width // 64), table).astype(np.float32)


def place_index(y, x, z):
    return ((y % RING) * RING + x % RING) * RING + z % RING


def shift(value, dy=0, dx=0, dz=0):
    pairs = [
        (place_index(y, x, z), place_index(y + dy, x + dx, z + dz))
        for y in range(RING)
        for x in range(RING)
        for z in range(RING)
    ]
    return lax.ppermute(value, "fsdp", pairs)


def narrow(value):
    return value.astype(jnp.float16)


def wide(value):
    return value.astype(jnp.float32)


FAR_UP, FAR_DOWN = ((2, 0), (2, 1)), ((2, 2), (2, 3))
UP, DOWN, OWN = (tuple((d, j) for j in range(RING)) for d in (1, 3, 0))


def places(half, block):
    return block[::-1] if half == 0 else block


def product_kernel(plan, a_ref, g_ref, *refs):
    outs, (held, turned, raw, sems, g_sem) = refs[: len(plan)], refs[len(plan) :]
    width = held.shape[2]
    cut = turned.shape[0] // 2
    place = lax.axis_index("fsdp")
    y, x, z = place >> 4, (place >> 2) & 3, place & 3
    order = list(dict.fromkeys(places(half, block) for half, blocks in plan for block in blocks))

    def fetch(slot):
        up_y, up_x = order[slot]
        start = pl.multiple_of((((y + up_y) & 3) * RING + ((x + up_x) & 3)) * width, width)
        return pltpu.make_async_copy(
            a_ref.at[:, pl.ds(start, width)], held.at[slot], sems.at[slot]
        )

    bring = pltpu.make_async_copy(g_ref, raw, g_sem)
    bring.start()
    for slot in range(len(order)):
        fetch(slot).start()
    bring.wait()
    turned[...] = raw[...].T * SCALE
    ready = 0
    for out, (half, blocks) in zip(outs, plan):
        part = turned[half * cut : (half + 1) * cut]
        for k, block in enumerate(blocks):
            slot = order.index(places(half, block))
            while ready <= slot:
                fetch(ready).wait()
                ready += 1
            product = jnp.dot(part, held[slot], preferred_element_type=jnp.float32)
            for to in range(RING):
                out[k, to ^ z] = product[:, to * 128 : (to + 1) * 128]


def products(activations, out_grads, *kinds, vmem):
    plan = [(half, blocks) for half in (0, 1) for blocks in kinds]
    depth, rows = activations.shape
    width, cut = rows // RING**2, out_grads.shape[1] // 2
    count = len({places(half, block) for half, blocks in plan for block in blocks})
    total = sum(len(blocks) for _, blocks in plan)
    outs = pl.pallas_call(
        functools.partial(product_kernel, plan),
        in_specs=[pl.BlockSpec(memory_space=pl.ANY)] * 2,
        out_specs=[pl.BlockSpec(memory_space=pltpu.VMEM)] * len(plan),
        out_shape=[
            jax.ShapeDtypeStruct((len(blocks), RING, cut, width // RING), jnp.float32)
            for _, blocks in plan
        ],
        scratch_shapes=[
            pltpu.VMEM((count, depth, width), activations.dtype),
            pltpu.VMEM(out_grads.shape[::-1], out_grads.dtype),
            pltpu.VMEM(out_grads.shape, out_grads.dtype),
            pltpu.SemaphoreType.DMA((count,)),
            pltpu.SemaphoreType.DMA,
        ],
        compiler_params=pltpu.CompilerParams(vmem_limit_bytes=vmem << 20),
        cost_estimate=pl.CostEstimate(
            flops=2 * total * width * cut * depth,
            bytes_accessed=count * depth * width * 2,
            transcendentals=0,
        ),
    )(activations, out_grads)
    return outs[: len(kinds)], outs[len(kinds) :]


def block_sum(terms, k):
    out = wide(terms[0][k])
    for value in terms[1:]:
        out = out + wide(value[k])
    return out


def scattered_grad(activations, out_grads):
    halves = (0, 1)
    far = products(activations, out_grads, FAR_UP, FAR_DOWN, vmem=49)
    near = products(activations, out_grads, UP, DOWN, vmem=44)
    own = products(activations, out_grads, OWN, vmem=44)

    def along(half, value, d):
        return shift(value, dx=d) if half == 0 else shift(value, dy=d)

    def across(half, value, d):
        return shift(value, dy=d) if half == 0 else shift(value, dx=d)

    first = [(along(h, narrow(far[h][0]), 1), along(h, narrow(far[h][1]), -1)) for h in halves]
    sums = []
    for h in halves:
        up, down = near[h]
        below, above = first[h]
        pads = ((0, 0, 0),) * 3
        zero = jnp.zeros((), jnp.float16)
        up = narrow(up + wide(lax.pad(below, zero, ((0, 2, 0),) + pads)))
        down = narrow(down + wide(lax.pad(above, zero, ((2, 0, 0),) + pads)))
        terms = own[h][0], along(h, up, 1), along(h, down, -1)
        sent = [across(h, narrow(block_sum(terms, d)), d) for d in ((2, 1, 3), (1, 3, 2))[h]]
        terms = [block_sum(terms, 0)] + sent
        sent = []
        for flip in (2, 3, 1):
            pairs = [(k, k ^ flip) for k in range(RING**3)]
            sent.append(lax.ppermute(narrow(block_sum(terms, flip)), "fsdp", pairs))
        out = block_sum(terms, 0)
        for value in sent:
            out = out + wide(value)
        sums.append(out)
    return sums


def moments(left, right, one, two):
    grad = jnp.concatenate([left[...], right[...]]).T * (1.0 / SCALE)
    return 0.8 * one[...] + 0.2 * grad, 0.95 * two[...] + 0.05 * grad * grad


def moment_kernel(left, right, one, two, new_one, new_two):
    new_one[...], new_two[...] = moments(left, right, one, two)


def band_kernel(left, right, one, two, drift, base, rows, cols, coeff):
    first, second = moments(left, right, one, two)
    step = first / (1.0 - 0.8**10) / (jnp.sqrt(second / (1.0 - 0.95**10)) + 1e-08)
    theta = base[...] + drift[...]
    delta = base[...] - (theta - 0.3 * (step + 0.1 * theta))
    inner = jnp.dot(rows[...], delta, precision=HIGHEST, preferred_element_type=jnp.float32)
    coeff[...] = lax.dot_general(
        inner, cols[...], (((1,), (1,)), ((), ())), precision=HIGHEST,
        preferred_element_type=jnp.float32,
    )


def outer_kernel(here, there, base, moment, rows, cols, new_base, new_outer, band_ref, *scratch):
    base_part, outer_part, band_part, sems = scratch
    band = (here[...] + there[...]) / 4.0
    band_part[...] = band
    copies = [pltpu.make_async_copy(band_part, band_ref, sems.at[0])]
    copies[0].start()
    inner = lax.dot_general(
        rows[...], band, (((0,), (0,)), ((), ())), precision=HIGHEST,
        preferred_element_type=jnp.float32,
    )
    half = moment.shape[1] // 2
    for k in range(2):
        at, small = slice(k * half, (k + 1) * half), slice(k * half // 4, (k + 1) * half // 4)
        smooth = jnp.dot(
            inner[:, small], cols[small, at], precision=HIGHEST,
            preferred_element_type=jnp.float32,
        )
        outer = 0.9 * moment[:, at] + smooth
        outer_part[:, at] = outer
        base_part[:, at] = base[:, at] - 0.7 * (smooth + 0.9 * outer)
        for part, whole in ((outer_part, new_outer), (base_part, new_base)):
            copy = pltpu.make_async_copy(part.at[:, at], whole.at[:, at], sems.at[len(copies)])
            copy.start()
            copies.append(copy)
    for copy in copies:
        copy.wait()


def on_chip(kernel, shapes, *args, copies=0):
    return pl.pallas_call(
        kernel,
        in_specs=[pl.BlockSpec(memory_space=pltpu.VMEM)] * len(args),
        out_specs=[pl.BlockSpec(memory_space=pl.ANY if copies else pltpu.VMEM)] * len(shapes),
        out_shape=[jax.ShapeDtypeStruct(shape, jnp.float32) for shape in shapes],
        scratch_shapes=[pltpu.VMEM(shape, jnp.float32) for shape in shapes if copies]
        + [pltpu.SemaphoreType.DMA((copies,))] * (copies > 0),
        compiler_params=pltpu.CompilerParams(vmem_limit_bytes=8 << 20),
    )(*args)


def flipped_island(value, flip):
    return lax.ppermute(value, "island", [(k, k ^ flip) for k in range(4)])


def local(activations, out_grads, drift, moment_one, moment_two, base, outer_moment):
    rows, cols = block_basis(drift.shape[1]), block_basis(drift.shape[2])
    left, right = scattered_grad(activations, out_grads)
    full, small = drift.shape[1:], (rows.shape[0], cols.shape[0])
    state = left, right, moment_one[0], moment_two[0]
    (coeff,) = on_chip(band_kernel, [small], *state, drift[0], base, rows, cols)
    chip = coeff + flipped_island(coeff, 1)
    there = flipped_island(chip, 2)
    first, second = on_chip(moment_kernel, [full, full], *state)
    new_base, new_outer, band = on_chip(
        outer_kernel, [full, full, small], chip, there, base, outer_moment, rows, cols, copies=5
    )
    return (new_base, new_outer, band, first[None], second[None])


def solution(mesh):
    in_specs = (
        P(("island", "fsdp"), None),
        P(("island", "fsdp"), None),
        P("island", "fsdp", None),
        P("island", "fsdp", None),
        P("island", "fsdp", None),
        P("fsdp", None),
        P("fsdp", None),
    )
    out_specs = (
        P("fsdp", None),
        P("fsdp", None),
        P("fsdp", None),
        P("island", "fsdp", None),
        P("island", "fsdp", None),
    )
    return jax.shard_map(local, mesh=mesh, in_specs=in_specs, out_specs=out_specs, check_vma=False)
```

```python
import functools
import math

import jax
import jax.numpy as jnp
import numpy as np
from jax import lax
from jax.experimental import pallas as pl
from jax.experimental.pallas import tpu as pltpu
from jax.sharding import PartitionSpec as P

RING = 4
SCALE = 8.0
HIGHEST = lax.Precision.HIGHEST


def block_basis(width):
    freq, place = np.arange(16.0)[:, None], np.arange(64.0)[None, :]
    table = math.sqrt(2.0 / 64.0) * np.cos(math.pi * (2.0 * place + 1.0) * freq / 128.0)
    table[0] /= math.sqrt(2.0)
    return np.kron(np.eye(width // 64), table).astype(np.float32)


def place_index(y, x, z):
    return ((y % RING) * RING + x % RING) * RING + z % RING


def shift(value, dy=0, dx=0, dz=0):
    pairs = [
        (place_index(y, x, z), place_index(y + dy, x + dx, z + dz))
        for y in range(RING)
        for x in range(RING)
        for z in range(RING)
    ]
    return lax.ppermute(value, "fsdp", pairs)


def narrow(value):
    return value.astype(jnp.float16)


def wide(value):
    return value.astype(jnp.float32)


FAR_UP, FAR_DOWN = ((2, 0), (2, 1)), ((2, 2), (2, 3))
UP, DOWN, OWN = (tuple((d, j) for j in range(RING)) for d in (1, 3, 0))


def places(half, block):
    return block[::-1] if half == 0 else block


def product_kernel(plan, a_ref, g_ref, *refs):
    outs, (held, turned, raw, sems, g_sem) = refs[: len(plan)], refs[len(plan) :]
    width = held.shape[2]
    cut = turned.shape[0] // 2
    place = lax.axis_index("fsdp")
    y, x, z = place >> 4, (place >> 2) & 3, place & 3
    order = list(dict.fromkeys(places(half, block) for half, blocks in plan for block in blocks))

    def fetch(slot):
        up_y, up_x = order[slot]
        start = pl.multiple_of((((y + up_y) & 3) * RING + ((x + up_x) & 3)) * width, width)
        return pltpu.make_async_copy(
            a_ref.at[:, pl.ds(start, width)], held.at[slot], sems.at[slot]
        )

    bring = pltpu.make_async_copy(g_ref, raw, g_sem)
    bring.start()
    for slot in range(len(order)):
        fetch(slot).start()
    bring.wait()
    turned[...] = raw[...].T * SCALE
    ready = 0
    for out, (half, blocks) in zip(outs, plan):
        part = turned[half * cut : (half + 1) * cut]
        for k, block in enumerate(blocks):
            slot = order.index(places(half, block))
            while ready <= slot:
                fetch(ready).wait()
                ready += 1
            product = jnp.dot(part, held[slot], preferred_element_type=jnp.float32)
            for to in range(RING):
                out[k, to ^ z] = product[:, to * 128 : (to + 1) * 128]


def products(activations, out_grads, *kinds, vmem):
    plan = [(half, blocks) for half in (0, 1) for blocks in kinds]
    depth, rows = activations.shape
    width, cut = rows // RING**2, out_grads.shape[1] // 2
    count = len({places(half, block) for half, blocks in plan for block in blocks})
    total = sum(len(blocks) for _, blocks in plan)
    outs = pl.pallas_call(
        functools.partial(product_kernel, plan),
        in_specs=[pl.BlockSpec(memory_space=pl.ANY)] * 2,
        out_specs=[pl.BlockSpec(memory_space=pltpu.VMEM)] * len(plan),
        out_shape=[
            jax.ShapeDtypeStruct((len(blocks), RING, cut, width // RING), jnp.float32)
            for _, blocks in plan
        ],
        scratch_shapes=[
            pltpu.VMEM((count, depth, width), activations.dtype),
            pltpu.VMEM(out_grads.shape[::-1], out_grads.dtype),
            pltpu.VMEM(out_grads.shape, out_grads.dtype),
            pltpu.SemaphoreType.DMA((count,)),
            pltpu.SemaphoreType.DMA,
        ],
        compiler_params=pltpu.CompilerParams(vmem_limit_bytes=vmem << 20),
        cost_estimate=pl.CostEstimate(
            flops=2 * total * width * cut * depth,
            bytes_accessed=count * depth * width * 2,
            transcendentals=0,
        ),
    )(activations, out_grads)
    return outs[: len(kinds)], outs[len(kinds) :]


def block_sum(terms, k):
    out = wide(terms[0][k])
    for value in terms[1:]:
        out = out + wide(value[k])
    return out


def crossing(value, flip):
    return lax.ppermute(value, "fsdp", [(k, k ^ flip) for k in range(RING**3)])


def scattered_grad(activations, out_grads):
    halves = (0, 1)
    far = products(activations, out_grads, FAR_UP, FAR_DOWN, vmem=49)
    near = products(activations, out_grads, UP, DOWN, vmem=44)
    own = products(activations, out_grads, OWN, vmem=44)

    def along(half, value, d):
        return shift(value, dx=d) if half == 0 else shift(value, dy=d)

    def across(half, value, d):
        return shift(value, dy=d) if half == 0 else shift(value, dx=d)

    first = [(along(h, narrow(far[h][0]), 1), along(h, narrow(far[h][1]), -1)) for h in halves]
    sums = []
    for h in halves:
        up, down = near[h]
        below, above = first[h]
        pads = ((0, 0, 0),) * 3
        zero = jnp.zeros((), jnp.float16)
        up = narrow(up + wide(lax.pad(below, zero, ((0, 2, 0),) + pads)))
        down = narrow(down + wide(lax.pad(above, zero, ((2, 0, 0),) + pads)))
        terms = own[h][0], along(h, up, 1), along(h, down, -1)
        sent = [across(h, narrow(block_sum(terms, d)), d) for d in (1, 3, 2)]
        terms = [block_sum(terms, 0)] + sent
        if h == 0:
            sent = [crossing(narrow(block_sum(terms, flip)), flip) for flip in (2, 3, 1)]
            out = block_sum(terms, 0)
        else:
            pair = narrow(jnp.stack([block_sum(terms, 1), block_sum(terms, 3)]))
            pair = crossing(pair, 1)
            sent = [pair[0], crossing(narrow(block_sum(terms, 2) + wide(pair[1])), 2)]
            out = block_sum(terms, 0)
        for value in sent:
            out = out + wide(value)
        sums.append(out)
    return sums


def moments(left, right, one, two):
    grad = jnp.concatenate([left[...], right[...]]).T * (1.0 / SCALE)
    return 0.8 * one[...] + 0.2 * grad, 0.95 * two[...] + 0.05 * grad * grad


def moment_kernel(left, right, one, two, new_one, new_two):
    new_one[...], new_two[...] = moments(left, right, one, two)


def band_kernel(left, right, one, two, drift, base, rows, cols, coeff):
    first, second = moments(left, right, one, two)
    step = first / (1.0 - 0.8**10) / (jnp.sqrt(second / (1.0 - 0.95**10)) + 1e-08)
    theta = base[...] + drift[...]
    delta = base[...] - (theta - 0.3 * (step + 0.1 * theta))
    inner = jnp.dot(rows[...], delta, precision=HIGHEST, preferred_element_type=jnp.float32)
    coeff[...] = lax.dot_general(
        inner, cols[...], (((1,), (1,)), ((), ())), precision=HIGHEST,
        preferred_element_type=jnp.float32,
    )


def outer_kernel(here, there, base, moment, rows, cols, new_base, new_outer, band_ref):
    band = (here[...] + there[...]) / 4.0
    band_ref[...] = band
    inner = lax.dot_general(
        rows[...], band, (((0,), (0,)), ((), ())), precision=HIGHEST,
        preferred_element_type=jnp.float32,
    )
    smooth = jnp.dot(inner, cols[...], precision=HIGHEST, preferred_element_type=jnp.float32)
    outer = 0.9 * moment[...] + smooth
    new_outer[...] = outer
    new_base[...] = base[...] - 0.7 * (smooth + 0.9 * outer)


def on_chip(kernel, shapes, *args):
    return pl.pallas_call(
        kernel,
        in_specs=[pl.BlockSpec(memory_space=pltpu.VMEM)] * len(args),
        out_specs=[pl.BlockSpec(memory_space=pltpu.VMEM)] * len(shapes),
        out_shape=[jax.ShapeDtypeStruct(shape, jnp.float32) for shape in shapes],
        compiler_params=pltpu.CompilerParams(vmem_limit_bytes=8 << 20),
    )(*args)


def flipped_island(value, flip):
    return lax.ppermute(value, "island", [(k, k ^ flip) for k in range(4)])


def local(activations, out_grads, drift, moment_one, moment_two, base, outer_moment):
    rows, cols = block_basis(drift.shape[1]), block_basis(drift.shape[2])
    left, right = scattered_grad(activations, out_grads)
    full, small = drift.shape[1:], (rows.shape[0], cols.shape[0])
    state = left, right, moment_one[0], moment_two[0]
    (coeff,) = on_chip(band_kernel, [small], *state, drift[0], base, rows, cols)
    chip = coeff + flipped_island(coeff, 1)
    there = flipped_island(chip, 2)
    first, second = on_chip(moment_kernel, [full, full], *state)
    new_base, new_outer, band = on_chip(
        outer_kernel, [full, full, small], chip, there, base, outer_moment, rows, cols
    )
    return (new_base, new_outer, band, first[None], second[None])


def solution(mesh):
    in_specs = (
        P(("island", "fsdp"), None),
        P(("island", "fsdp"), None),
        P("island", "fsdp", None),
        P("island", "fsdp", None),
        P("island", "fsdp", None),
        P("fsdp", None),
        P("fsdp", None),
    )
    out_specs = (
        P("fsdp", None),
        P("fsdp", None),
        P("fsdp", None),
        P("island", "fsdp", None),
        P("island", "fsdp", None),
    )
    return jax.shard_map(local, mesh=mesh, in_specs=in_specs, out_specs=out_specs, check_vma=False)
```
